32 devices in a mesh: ctx: 8 (over y, x, core), head: 4 (over z).
Axes of the slice: x: 2, y: 2, z: 4, core: 2. Of those that a mesh axis runs over, the one named last changes fastest.
Arguments:
- query_heads: bfloat16 [128, 128, 192], P('ctx', 'head'), may hold values from -6 to 6
- absorb_up: bfloat16 [128, 128, 512], P('head'), may hold values from -0.5 to 0.5
- latent_keys: bfloat16 [8192, 576], P('ctx'), may hold values from -6 to 6
- lse_heads: float32 [128, 128], P(None, 'head'), as said below
- index_query: bfloat16 [128, 64, 128], P('ctx', 'head'), may hold values from -6 to 6
- index_weight: bfloat16 [128, 64], P('ctx', 'head'), may hold values from -0.75 to 0.75
- index_keys: bfloat16 [8192, 128], P('ctx'), may hold values from -6 to 6
- lse_index: float32 [128], replicated, as said below
- query_pos: int32 [128], replicated, may hold values from 0 to 8191, as said below
- key_blocks: int32 [8], P('ctx'), may hold values from 0 to 7, each once
Outputs:
- query_grad: float32 [128, 64, 128], P('ctx', 'head')
- key_grad: float32 [8192, 128], P(('ctx', 'head'))
The draws below stay inside these ranges and needn't reach their ends.
Inputs may be any that keep to these rules, and one draw needn't show every extreme that they name: `query_pos`: positions of the queries in a causal sequence of 8192 tokens. `key_blocks`: each index of ctx holds the 1024 keys of one block of the sequence, every block once. `lse_heads`: saved log-sum-exp values of the attention heads. `lse_index`: saved log normalizers of the indexer.
All inputs are finite; a program needn't handle non-finite values.
Results may differ from the reference program's by a relative error of at most 0.0094.
Values may be sent and summed in bfloat16 or wider, within the bound.
No kernel may reach another device: no remote copies, remote signals or barrier semaphores. Data moves between devices by JAX's collectives and lax.ppermute only.
A program may use at most 64 MiB of HBM per device.

```python
import jax
import jax.numpy as jnp
from jax import lax

HEADS = 128
DN = 128
DC = 512
IHEADS = 64
DI = 128
KEY_DEV = 1024
QUERIES = 128
DQ = 192
DL = 576
KEYS = 8192
N_CTX = 8


def positions(key):
    return jax.random.randint(jax.random.fold_in(key, 11), (QUERIES,), 0, KEYS).astype(jnp.int32)


def draw_query_pos(key, part):
    return positions(key)


def draw_lse_heads(key, part):
    counts = positions(key).astype(jnp.float32) + 1.0
    noise = jax.random.uniform(jax.random.fold_in(key, 23), (QUERIES, HEADS), jnp.float32)
    return jnp.log(counts)[:, None] + 1.0 + noise


def draw_lse_index(key, part):
    counts = positions(key).astype(jnp.float32) + 1.0
    noise = jax.random.uniform(jax.random.fold_in(key, 37), (QUERIES,), jnp.float32)
    return jnp.log(counts) + 0.5 * noise


def shard_levels(key, shape, cuts, low, top_value):
    def one(dim, blocks):
        heights = jax.random.uniform(jax.random.fold_in(jax.random.fold_in(key, 6), dim), (blocks,), jnp.float32, low / len(cuts), top_value / len(cuts))
        return jnp.repeat(jnp.exp(heights), shape[dim] // blocks).reshape((-1,) + (1,) * (len(shape) - dim - 1))

    level = one(*cuts[0])
    for cut in cuts[1:]:
        level = level * one(*cut)
    return level


def gaussian(stream_key, dims, width, reach, split=(), kind=jnp.bfloat16):
    array = width * jax.random.normal(stream_key, dims, jnp.float32)
    if split:
        array = array * shard_levels(stream_key, dims, split, -0.22, 0.18)
    return jnp.clip(array, -reach, reach).astype(kind)


def setup_inputs(seed: int = 0) -> dict:
    key_of = jax.random.split(jax.random.key(seed), 11)
    return {
        "query_heads": gaussian(key_of[0], (QUERIES, HEADS, DQ), 1.0, 6.0, ((0, 8), (1, 4))),
        "absorb_up": gaussian(key_of[1], (HEADS, DN, DC), DN ** -0.5, 0.5, ((0, 4),)),
        "latent_keys": gaussian(key_of[2], (KEYS, DL), 1.0, 6.0, ((0, 8),)),
        "lse_heads": draw_lse_heads(jax.random.fold_in(key_of[10], 71), 0),
        "index_query": gaussian(key_of[4], (QUERIES, IHEADS, DI), 1.0, 6.0, ((0, 8), (1, 4))),
        "index_weight": gaussian(key_of[5], (QUERIES, IHEADS), IHEADS ** -0.5, 0.75, ((0, 8), (1, 4))),
        "index_keys": gaussian(key_of[6], (KEYS, DI), 1.0, 6.0, ((0, 8),)),
        "lse_index": draw_lse_index(jax.random.fold_in(key_of[10], 71), 0),
        "query_pos": draw_query_pos(jax.random.fold_in(key_of[10], 71), 0),
        "key_blocks": jax.random.permutation(key_of[9], N_CTX).astype(jnp.int32),
    }


def reference(query_heads, absorb_up, latent_keys, lse_heads, index_query, index_weight, index_keys, lse_index, query_pos, key_blocks):
    key_pos = (jnp.repeat(key_blocks, KEY_DEV) * KEY_DEV + jnp.tile(jnp.arange(KEY_DEV, dtype=jnp.int32), N_CTX)).astype(jnp.int32)
    visible = key_pos[None, :] <= query_pos[:, None]
    nope_part = jnp.einsum("qhn,hnc->qhc", query_heads[:, :, :DN].astype(jnp.float32), absorb_up.astype(jnp.float32)).astype(jnp.bfloat16)
    absorbed = jnp.concatenate([nope_part, query_heads[:, :, DN:]], axis=2)
    attn_scale = DQ ** -0.5

    def head_step(running, items):
        q_head, lse_col = items
        scores = jnp.dot(q_head, latent_keys.T, preferred_element_type=jnp.float32) * attn_scale
        return running + jnp.where(visible, jnp.exp(scores - lse_col[:, None]), 0.0), None

    prob_sum = lax.scan(head_step, jnp.zeros((QUERIES, KEYS), jnp.float32), (jnp.swapaxes(absorbed, 0, 1), lse_heads.T))[0]
    row_total = jnp.sum(prob_sum, axis=1)
    target = prob_sum / row_total[:, None]
    index_scale = DI ** -0.5
    query_rows = jnp.swapaxes(index_query, 0, 1)
    weight_rows = index_weight.T.astype(jnp.float32)

    def logit_step(running, items):
        one_query, one_weight = items
        scores = jnp.dot(one_query, index_keys.T, preferred_element_type=jnp.float32) * index_scale
        return running + one_weight[:, None] * jax.nn.relu(scores), None

    logits = lax.scan(logit_step, jnp.zeros((QUERIES, KEYS), jnp.float32), (query_rows, weight_rows))[0]
    index_prob = jnp.where(visible, jnp.exp(logits - lse_index[:, None]), 0.0)
    d_logit = KEYS ** 0.5 * (index_prob - target)

    def grad_step(key_total, items):
        one_query, one_weight = items
        scores = jnp.dot(one_query, index_keys.T, preferred_element_type=jnp.float32) * index_scale
        d_score = jnp.where(scores > 0.0, one_weight[:, None] * d_logit, 0.0).astype(jnp.bfloat16)
        one_grad = jnp.dot(d_score, index_keys, preferred_element_type=jnp.float32) * index_scale
        key_total = key_total + jnp.dot(d_score.T, one_query, preferred_element_type=jnp.float32) * index_scale
        return key_total, one_grad

    key_grad, query_parts = lax.scan(grad_step, jnp.zeros((KEYS, DI), jnp.float32), (query_rows, weight_rows))
    query_grad = jnp.swapaxes(query_parts, 0, 1)
    return query_grad, key_grad
```

```python
import functools
import math

import jax
import jax.numpy as jnp
from jax import lax
from jax.experimental import pallas as pl
from jax.experimental.pallas import tpu as pltpu
from jax.sharding import PartitionSpec as P

LOG2E = math.log2(math.e)
F32 = jnp.float32
BF16 = jnp.bfloat16
LANES = 128
VMEM_LIMIT = 48 * 1024 * 1024


def matmul(lhs, rhs):
    return jnp.dot(lhs, rhs, preferred_element_type=F32)


def send(array, axis, size, offset):
    return lax.ppermute(array, axis, [(i, i ^ offset) for i in range(size)])


def call(kernel, out_shape, **options):
    return pl.pallas_call(
        kernel,
        out_shape=out_shape,
        compiler_params=pltpu.CompilerParams(vmem_limit_bytes=VMEM_LIMIT),
        **options,
    )


def vmem():
    return pl.BlockSpec(memory_space=pltpu.VMEM)


def smem():
    return pl.BlockSpec(memory_space=pltpu.SMEM)


def flip(row, offset, chunk):
    width = row.shape[1]
    block = lax.broadcasted_iota(jnp.int32, row.shape, 1) // chunk
    bit = 0
    while offset >> bit:
        if (offset >> bit) & 1:
            stride = width // (2 * chunk) if bit == 0 else 1 << (bit - 1)
            ahead = pltpu.roll(row, width - stride * chunk, 1)
            back = pltpu.roll(row, stride * chunk, 1)
            row = jnp.where((block // stride) % 2 == 0, ahead, back)
        bit += 1
    return row


def in_local_order(blocks, me):
    ctx, tail = blocks.shape[0], blocks.shape[1:]
    stride = 1
    while stride < ctx:
        swapped = blocks.reshape((-1, 2, stride) + tail)[:, ::-1].reshape(blocks.shape)
        blocks = jnp.where((me // stride) % 2 == 1, swapped, blocks)
        stride *= 2
    return jnp.swapaxes(blocks.reshape((ctx // 2, 2) + tail), 0, 1).reshape(blocks.shape)


def logit_kernel(iq_a, iq_b, w_a, w_b, keys_t, out, rows):
    count = out.shape[0]
    depth = keys_t.shape[0]
    heads = iq_a.shape[1] // depth
    scale = depth ** -0.5
    weight = jnp.concatenate([w_a[...], w_b[...]], axis=0).astype(F32) * scale
    for j in range(heads):
        part = slice(j * depth, (j + 1) * depth)
        rows[j * count : (j + 1) * count, :] = jnp.concatenate([iq_a[:, part], iq_b[:, part]], axis=0)
    width = 256
    for first in range(0, keys_t.shape[1], width):
        cols = slice(first, first + width)
        score = matmul(rows[...], keys_t[:, cols])
        total = None
        for j in range(heads):
            term = weight[:, j : j + 1] * jnp.maximum(score[j * count : (j + 1) * count], 0.0)
            total = term if total is None else total + term
        out[:, cols] = total


def prob_kernel(scale, info, na, nb, ra, rb, up, keys_t, lse, pos, *rest):
    outs, row_sum, lhs, acc = rest[:-3], rest[-3], rest[-2], rest[-1]
    step = pl.program_id(0)
    group, depth, latent = up.shape
    count, keys = acc.shape
    rope = ra.shape[1] // group
    for i in range(group):
        part = slice(i * depth, (i + 1) * depth)
        query = jnp.concatenate([na[:, part], nb[:, part]], axis=0)
        lhs[i * count : (i + 1) * count, :latent] = matmul(query, up[i]).astype(BF16)
        low = (i * rope // LANES) * LANES
        pair = jnp.concatenate([ra[:, low : low + LANES], rb[:, low : low + LANES]], axis=0)
        shift = i * rope - low
        if shift:
            pair = jnp.concatenate([pair[:, shift:], pair[:, :shift]], axis=1)
        lhs[i * count : (i + 1) * count, latent:] = pair

    width = 256
    for first in range(0, keys, width):
        cols = slice(first, first + width)
        score = matmul(lhs[...], keys_t[:, cols])
        total = None
        for i in range(group):
            term = jnp.exp2(score[i * count : (i + 1) * count] * (scale * LOG2E) - lse[0, :, i : i + 1])
            total = term if total is None else total + term

        @pl.when(step == 0)
        def _():
            acc[:, cols] = total

        @pl.when(step > 0)
        def _():
            acc[:, cols] += total

    @pl.when(step == pl.num_programs(0) - 1)
    def _():
        key_pos = info[0] * keys + lax.broadcasted_iota(jnp.int32, (count, keys), 1)
        masked = jnp.where(key_pos <= pos[...], acc[...], 0.0)
        acc[...] = masked
        total = jnp.sum(masked, axis=1, keepdims=True)
        row_sum[...] = jnp.transpose(jnp.broadcast_to(total, (count, count)))[:8]
        size = count // len(outs)
        for k, out in enumerate(outs):
            start = pl.multiple_of(jnp.bitwise_xor(info[1], k) * size, size)
            out[...] = acc[pl.ds(start, size), :].astype(BF16)


def add_swapped_kernel(chunk, mine, other, out):
    out[...] = mine[...] + flip(other[...], 1, chunk)


def merge_kernel(chunk, peers, offsets, *refs):
    slices, totals, out = refs[:peers], refs[peers:-1], refs[-1]
    size = slices[0].shape[0]
    total = slices[0][...].astype(F32)
    for ref in slices[1:]:
        total = total + ref[...].astype(F32)
    out[:size, :] = total.astype(BF16)
    row = totals[0][...]
    for offset, ref in zip(offsets, totals[1:]):
        row = row + flip(ref[...], offset, chunk)
    row = jnp.concatenate([row, row], axis=0)
    width = row.shape[1]
    out[size:, :] = jnp.zeros((out.shape[0] - size, out.shape[1]), BF16)
    for i in range(3):
        piece = row.astype(BF16)
        out[size:, i * width : (i + 1) * width] = piece
        row = row - piece.astype(F32)


def grad_kernel(loss_scale, peers, info, *refs):
    slices = refs[:peers]
    logits, iq_a, iq_b, w_a, w_b, index_keys, keys_t, lse, pos = refs[peers : peers + 9]
    keep, away = refs[peers + 9 : peers + 11]
    dk_outs = refs[peers + 11 : 2 * peers + 11]
    rows, prob, dk = refs[2 * peers + 11 :]
    count, keys = logits.shape
    depth = keys_t.shape[0]
    heads = iq_a.shape[1] // depth
    half = count // 2
    scale = depth ** -0.5
    size = count // peers
    total = None
    for k, ref in enumerate(slices):
        start = pl.multiple_of(jnp.bitwise_xor(info[1], k) * size, size)
        prob[pl.ds(start, size), :] = ref[:size, :].astype(F32)
        for i in range(3):
            piece = ref[size : size + 16, i * count : (i + 1) * count].astype(F32)
            total = piece if total is None else total + piece
    square = (count, count)
    diagonal = lax.broadcasted_iota(jnp.int32, square, 0) == lax.broadcasted_iota(jnp.int32, square, 1)
    row_total = jnp.sum(
        jnp.where(diagonal, jnp.broadcast_to(total[:1], square), 0.0), axis=1, keepdims=True
    )
    key_pos = info[0] * keys + lax.broadcasted_iota(jnp.int32, (count, keys), 1)
    index_prob = jnp.where(key_pos <= pos[...], jnp.exp(logits[...] - lse[...]), 0.0)
    prob[...] = loss_scale * (index_prob - prob[...] / row_total)

    weight = jnp.concatenate([w_a[...], w_b[...]], axis=0).astype(F32)
    for j in range(heads):
        part = slice(j * depth, (j + 1) * depth)
        rows[j * count : (j + 1) * count, :] = jnp.concatenate([iq_a[:, part], iq_b[:, part]], axis=0)
    group = min(4, heads)
    for first in range(0, heads, group):
        mine = rows[first * count : (first + group) * count, :]
        score = matmul(mine, keys_t[...])
        d_score = jnp.concatenate(
            [
                jnp.where(
                    score[i * count : (i + 1) * count] > 0.0,
                    weight[:, first + i : first + i + 1] * prob[...],
                    0.0,
                ).astype(BF16)
                for i in range(group)
            ],
            axis=0,
        )
        dq = matmul(d_score, index_keys[...]) * scale
        for i in range(group):
            part = slice((first + i) * depth, (first + i + 1) * depth)
            keep[:, part] = dq[i * count : i * count + half]
            away[:, part] = dq[i * count + half : (i + 1) * count].astype(BF16)
        term = lax.dot_general(d_score, mine, (((0,), (0,)), ((), ())), preferred_element_type=F32)
        if first == 0:
            dk[...] = term
        else:
            dk[...] += term
    size = keys // peers
    for k, out in enumerate(dk_outs):
        start = pl.multiple_of(jnp.bitwise_xor(info[1], k) * size, size)
        out[...] = (dk[pl.ds(start, size), :] * scale).astype(out.dtype)


def fold_kernel(keep, other, own, *outs):
    chunk = own.shape[0]
    total = keep[...] + other[...].astype(F32)
    own[...] = total[:chunk]
    for i, out in enumerate(outs):
        out[...] = total[(i + 1) * chunk : (i + 2) * chunk].astype(BF16)


def final_kernel(chunks, *refs):
    parts, dk_parts, (dq_out, dk_out) = refs[:chunks], refs[chunks:-2], refs[-2:]
    total = parts[0][...]
    for ref in parts[1:]:
        total = total + ref[...].astype(F32)
    depth = dq_out.shape[2]
    for j in range(dq_out.shape[1]):
        dq_out[:, j, :] = total[:, j * depth : (j + 1) * depth]
    dk = dk_parts[0][...]
    for ref in dk_parts[1:]:
        dk = dk + ref[...].astype(F32)
    dk_out[...] = dk


def body(
    ctx,
    peers,
    query_heads,
    absorb_up,
    latent_keys,
    lse_heads,
    index_query,
    index_weight,
    index_keys,
    lse_index,
    query_pos,
    key_blocks,
):
    chunk, heads, width = query_heads.shape
    _, nope, latent = absorb_up.shape
    rope = width - nope
    keys = latent_keys.shape[0]
    index_heads, depth = index_query.shape[1:]
    count = chunk * ctx
    half = count // 2
    me = lax.axis_index("ctx")
    info = jnp.stack([key_blocks[0], lax.axis_index("head").astype(jnp.int32)])
    evens = list(range(2, ctx, 2))

    payload = jnp.concatenate(
        [
            query_heads[:, :, :nope].reshape(chunk, -1),
            query_heads[:, :, nope:].reshape(chunk, -1),
            index_query.reshape(chunk, -1),
            jnp.pad(index_weight, ((0, 0), (0, LANES - index_heads))),
        ],
        axis=1,
    )
    side_a = jnp.concatenate([payload] + [send(payload, "ctx", ctx, k) for k in evens], axis=0)
    side_b = send(side_a, "ctx", ctx, 1)

    local = jnp.concatenate(
        [lse_heads * LOG2E, lse_index[:, None], query_pos.astype(F32)[:, None]], axis=1
    )
    local = in_local_order(local.reshape(ctx, chunk, -1), me).reshape(count, -1)
    group = min(8, heads)
    steps = heads // group
    lse_groups = jnp.swapaxes(local[:, :heads].reshape(count, steps, group), 0, 1)
    lse_column = local[:, heads : heads + 1]
    pos_column = local[:, heads + 1 : heads + 2].astype(jnp.int32)

    latent_t = jnp.pad(latent_keys, ((0, 0), (0, LANES - rope))).T
    index_t = index_keys.T

    iq_width = index_heads * depth
    iq_spec = pl.BlockSpec((half, iq_width), lambda *_: (0, heads * width // iq_width))
    w_spec = pl.BlockSpec((half, LANES), lambda *_: (0, (heads * width + iq_width) // LANES))
    logit_part = call(
        logit_kernel,
        jax.ShapeDtypeStruct((count, keys), F32),
        grid=(1,),
        in_specs=[iq_spec, iq_spec, w_spec, w_spec, vmem()],
        out_specs=vmem(),
        scratch_shapes=[pltpu.VMEM((index_heads * count, depth), BF16)],
    )(side_a, side_b, side_a, side_b, index_t)
    logits = lax.psum(logit_part, "head")

    rope_first = heads * nope // (group * rope)
    nope_spec = pl.BlockSpec((half, group * nope), lambda g: (0, g))
    rope_spec = pl.BlockSpec((half, group * rope), lambda g: (0, rope_first + g))
    slice_shape = jax.ShapeDtypeStruct((count // peers, keys), BF16)
    *slices, row_sum = call(
        functools.partial(prob_kernel, width ** -0.5),
        [slice_shape] * peers + [jax.ShapeDtypeStruct((8, count), F32)],
        grid=(steps,),
        in_specs=[
            smem(),
            nope_spec,
            nope_spec,
            rope_spec,
            rope_spec,
            pl.BlockSpec((group, nope, latent), lambda g: (g, 0, 0)),
            vmem(),
            pl.BlockSpec((1, count, group), lambda g: (g, 0, 0)),
            vmem(),
        ],
        out_specs=[vmem()] * (peers + 1),
        scratch_shapes=[
            pltpu.VMEM((group * count, latent + LANES), BF16),
            pltpu.VMEM((count, keys), F32),
        ],
    )(info, side_a, side_b, side_a, side_b, absorb_up, latent_t, lse_groups, pos_column)

    row_sum = call(
        functools.partial(add_swapped_kernel, chunk),
        jax.ShapeDtypeStruct((8, count), F32),
    )(row_sum, send(row_sum, "ctx", ctx, 1))
    got = [slices[0]] + [send(slices[k], "head", peers, k) for k in range(1, peers)]
    totals = [row_sum] + [send(row_sum, "ctx", ctx, k) for k in evens]
    merged = call(
        functools.partial(merge_kernel, chunk, peers, evens),
        jax.ShapeDtypeStruct((count // peers + 16, keys), BF16),
    )(*got, *totals)
    gathered = [merged] + [send(merged, "head", peers, k) for k in range(1, peers)]

    loss_scale = (keys * ctx) ** 0.5
    dk_slice = (keys // peers, depth)
    outs = call(
        functools.partial(grad_kernel, loss_scale, peers),
        [
            jax.ShapeDtypeStruct((half, iq_width), F32),
            jax.ShapeDtypeStruct((half, iq_width), BF16),
            jax.ShapeDtypeStruct(dk_slice, F32),
        ]
        + [jax.ShapeDtypeStruct(dk_slice, BF16)] * (peers - 1),
        grid=(1,),
        in_specs=[smem()]
        + [vmem()] * peers
        + [vmem(), iq_spec, iq_spec, w_spec, w_spec, vmem(), vmem(), vmem(), vmem()],
        out_specs=[vmem()] * (peers + 2),
        scratch_shapes=[
            pltpu.VMEM((index_heads * count, depth), BF16),
            pltpu.VMEM((count, keys), F32),
            pltpu.VMEM((keys, depth), F32),
        ],
    )(
        info,
        *gathered,
        logits,
        side_a,
        side_b,
        side_a,
        side_b,
        index_keys,
        index_t,
        lse_column,
        pos_column,
    )
    keep, away, dk_own, *dk_away = outs
    other = send(away, "ctx", ctx, 1)
    dk_parts = [dk_own] + [send(dk_away[k - 1], "head", peers, k) for k in range(1, peers)]
    own, *parts = call(
        fold_kernel,
        [jax.ShapeDtypeStruct((chunk, iq_width), F32)]
        + [jax.ShapeDtypeStruct((chunk, iq_width), BF16)] * len(evens),
    )(keep, other)
    dq_parts = [own] + [send(part, "ctx", ctx, k) for part, k in zip(parts, evens)]
    return tuple(
        call(
            functools.partial(final_kernel, len(dq_parts)),
            [
                jax.ShapeDtypeStruct((chunk, index_heads, depth), F32),
                jax.ShapeDtypeStruct(dk_slice, F32),
            ],
        )(*dq_parts, *dk_parts)
    )


def solution(mesh):
    placed = (
        P("ctx", "head", None),
        P("head", None, None),
        P("ctx", None),
        P(None, "head"),
        P("ctx", "head", None),
        P("ctx", "head"),
        P("ctx", None),
        P(),
        P(),
        P("ctx"),
    )
    return jax.shard_map(
        functools.partial(body, mesh.shape["ctx"], mesh.shape["head"]),
        mesh=mesh,
        in_specs=placed,
        out_specs=(P("ctx", "head", None), P(("ctx", "head"), None)),
        check_vma=False,
    )
```

```python
import functools
import math

import jax
import jax.numpy as jnp
from jax import lax
from jax.experimental import pallas as pl
from jax.experimental.pallas import tpu as pltpu
from jax.sharding import PartitionSpec as P

LOG2E = math.log2(math.e)
F32 = jnp.float32
BF16 = jnp.bfloat16
LANES = 128
VMEM_LIMIT = 48 * 1024 * 1024


def matmul(lhs, rhs):
    return jnp.dot(lhs, rhs, preferred_element_type=F32)


def send(array, axis, size, offset):
    return lax.ppermute(array, axis, [(i, i ^ offset) for i in range(size)])


def swap_heads(slices, peers):
    return [slices[0]] + [send(slices[k], "head", peers, k) for k in range(1, peers)]


def call(kernel, out_shape, **options):
    return pl.pallas_call(
        kernel,
        out_shape=out_shape,
        compiler_params=pltpu.CompilerParams(vmem_limit_bytes=VMEM_LIMIT),
        **options,
    )


def vmem():
    return pl.BlockSpec(memory_space=pltpu.VMEM)


def smem():
    return pl.BlockSpec(memory_space=pltpu.SMEM)


def flip(row, offset, chunk):
    width = row.shape[1]
    block = lax.broadcasted_iota(jnp.int32, row.shape, 1) // chunk
    bit = 0
    while offset >> bit:
        if (offset >> bit) & 1:
            stride = width // (2 * chunk) if bit == 0 else 1 << (bit - 1)
            ahead = pltpu.roll(row, width - stride * chunk, 1)
            back = pltpu.roll(row, stride * chunk, 1)
            row = jnp.where((block // stride) % 2 == 0, ahead, back)
        bit += 1
    return row


def in_local_order(blocks, me):
    ctx, tail = blocks.shape[0], blocks.shape[1:]
    stride = 1
    while stride < ctx:
        swapped = blocks.reshape((-1, 2, stride) + tail)[:, ::-1].reshape(blocks.shape)
        blocks = jnp.where((me // stride) % 2 == 1, swapped, blocks)
        stride *= 2
    return jnp.swapaxes(blocks.reshape((ctx // 2, 2) + tail), 0, 1).reshape(blocks.shape)


def logit_kernel(info, iq_a, iq_b, w_a, w_b, keys_t, *rest):
    outs, rows, acc = rest[:-2], rest[-2], rest[-1]
    count = acc.shape[0]
    depth = keys_t.shape[0]
    heads = iq_a.shape[1] // depth
    scale = depth ** -0.5
    weight = jnp.concatenate([w_a[...], w_b[...]], axis=0).astype(F32) * scale
    for j in range(heads):
        part = slice(j * depth, (j + 1) * depth)
        rows[j * count : (j + 1) * count, :] = jnp.concatenate([iq_a[:, part], iq_b[:, part]], axis=0)
    group = min(4, heads)
    for first in range(0, heads, group):
        score = matmul(rows[first * count : (first + group) * count, :], keys_t[...])
        total = None
        for i in range(group):
            j = first + i
            term = weight[:, j : j + 1] * jnp.maximum(score[i * count : (i + 1) * count], 0.0)
            total = term if total is None else total + term
        if first == 0:
            acc[...] = total
        else:
            acc[...] += total
    size = count // len(outs)
    for k, out in enumerate(outs):
        start = pl.multiple_of(jnp.bitwise_xor(info[1], k) * size, size)
        out[...] = acc[pl.ds(start, size), :]


def prob_kernel(scale, info, na, nb, ra, rb, up, keys_t, lse, pos, *rest):
    outs, lhs, acc = rest[:-2], rest[-2], rest[-1]
    step = pl.program_id(0)
    group, depth, latent = up.shape
    count, keys = acc.shape
    rope = ra.shape[1] // group
    for i in range(group):
        part = slice(i * depth, (i + 1) * depth)
        query = jnp.concatenate([na[:, part], nb[:, part]], axis=0)
        lhs[i * count : (i + 1) * count, :latent] = matmul(query, up[i]).astype(BF16)
        low = (i * rope // LANES) * LANES
        pair = jnp.concatenate([ra[:, low : low + LANES], rb[:, low : low + LANES]], axis=0)
        shift = i * rope - low
        if shift:
            pair = jnp.concatenate([pair[:, shift:], pair[:, :shift]], axis=1)
        lhs[i * count : (i + 1) * count, latent:] = pair

    score = matmul(lhs[...], keys_t[...])
    total = None
    for i in range(group):
        term = jnp.exp2(score[i * count : (i + 1) * count] * (scale * LOG2E) - lse[0, :, i : i + 1])
        total = term if total is None else total + term

    @pl.when(step == 0)
    def _():
        acc[...] = total

    @pl.when(step > 0)
    def _():
        acc[...] += total

    @pl.when(step == pl.num_programs(0) - 1)
    def _():
        key_pos = info[0] * keys + lax.broadcasted_iota(jnp.int32, (count, keys), 1)
        masked = jnp.where(key_pos <= pos[...], acc[...], 0.0)
        acc[...] = masked
        total = jnp.sum(masked, axis=1, keepdims=True)
        size = count // len(outs)
        row = jnp.transpose(jnp.broadcast_to(total, (count, count)))[:size]
        line = lax.broadcasted_iota(jnp.int32, row.shape, 0)
        high = row.astype(BF16).astype(F32)
        middle = (row - high).astype(BF16).astype(F32)
        low = row - high - middle
        packed = jnp.where(line == 0, high, jnp.where(line == 1, middle, jnp.where(line == 2, low, 0.0)))
        for k, out in enumerate(outs):
            start = pl.multiple_of(jnp.bitwise_xor(info[1], k) * size, size)
            out[:, :keys] = acc[pl.ds(start, size), :].astype(BF16)
            out[:, keys:] = packed.astype(BF16)


def add_swapped_kernel(chunk, mine, other, out):
    out[...] = mine[...] + flip(other[...], 1, chunk)


def merge_kernel(*refs):
    slices, out, row_sum = refs[:-2], refs[-2], refs[-1]
    keys = out.shape[1]
    total = None
    for ref in slices:
        part = ref[...].astype(F32)
        total = part if total is None else total + part
    out[...] = total[:, :keys].astype(BF16)
    row = jnp.sum(total[:, keys:], axis=0, keepdims=True)
    row_sum[...] = jnp.broadcast_to(row, row_sum.shape)


def index_prob_kernel(info, lse, pos, *refs):
    slices, out = refs[:-1], refs[-1]
    size, keys = out.shape
    total = slices[0][...]
    for ref in slices[1:]:
        total = total + ref[...]
    rows = pl.ds(pl.multiple_of(info[1] * size, size), size)
    key_pos = info[0] * keys + lax.broadcasted_iota(jnp.int32, (size, keys), 1)
    out[...] = jnp.where(key_pos <= pos[rows, :], jnp.exp(total - lse[rows, :]), 0.0).astype(BF16)


def grad_kernel(loss_scale, chunk, peers, offsets, info, *refs):
    slices, refs = refs[:peers], refs[peers:]
    index_slices, refs = refs[:peers], refs[peers:]
    totals, refs = refs[: len(offsets) + 1], refs[len(offsets) + 1 :]
    iq_a, iq_b, w_a, w_b, index_keys, keys_t, keep, away = refs[:8]
    dk_outs, (rows, prob, dk) = refs[8:-3], refs[-3:]
    count, keys = prob.shape
    depth = keys_t.shape[0]
    heads = iq_a.shape[1] // depth
    half = count // 2
    scale = depth ** -0.5
    size = count // peers
    row = totals[0][...]
    for offset, ref in zip(offsets, totals[1:]):
        row = row + flip(ref[...], offset, chunk)
    square = (count, count)
    diagonal = lax.broadcasted_iota(jnp.int32, square, 0) == lax.broadcasted_iota(jnp.int32, square, 1)
    row_total = jnp.sum(jnp.where(diagonal, jnp.broadcast_to(row[:1], square), 0.0), axis=1, keepdims=True)
    prob[...] = jnp.broadcast_to(row_total, (count, keys))
    for k in range(peers):
        part = pl.ds(pl.multiple_of(jnp.bitwise_xor(info[1], k) * size, size), size)
        target = slices[k][...].astype(F32) / prob[part, :]
        prob[part, :] = loss_scale * (index_slices[k][...].astype(F32) - target)

    weight = jnp.concatenate([w_a[...], w_b[...]], axis=0).astype(F32)
    for j in range(heads):
        part = slice(j * depth, (j + 1) * depth)
        rows[j * count : (j + 1) * count, :] = jnp.concatenate([iq_a[:, part], iq_b[:, part]], axis=0)
    group = min(4, heads)
    for first in range(0, heads, group):
        mine = rows[first * count : (first + group) * count, :]
        score = matmul(mine, keys_t[...])
        d_score = jnp.concatenate(
            [
                jnp.where(
                    score[i * count : (i + 1) * count] > 0.0,
                    weight[:, first + i : first + i + 1] * prob[...],
                    0.0,
                ).astype(BF16)
                for i in range(group)
            ],
            axis=0,
        )
        dq = matmul(d_score, index_keys[...]) * scale
        for i in range(group):
            part = slice((first + i) * depth, (first + i + 1) * depth)
            keep[:, part] = dq[i * count : i * count + half]
            away[:, part] = dq[i * count + half : (i + 1) * count].astype(BF16)
        term = lax.dot_general(d_score, mine, (((0,), (0,)), ((), ())), preferred_element_type=F32)
        if first == 0:
            dk[...] = term
        else:
            dk[...] += term
    size = keys // peers
    for k, out in enumerate(dk_outs):
        start = pl.multiple_of(jnp.bitwise_xor(info[1], k) * size, size)
        out[...] = (dk[pl.ds(start, size), :] * scale).astype(out.dtype)


def fold_kernel(keep, other, own, *outs):
    chunk = own.shape[0]
    total = keep[...] + other[...].astype(F32)
    own[...] = total[:chunk]
    for i, out in enumerate(outs):
        out[...] = total[(i + 1) * chunk : (i + 2) * chunk].astype(BF16)


def final_kernel(chunks, *refs):
    parts, dk_parts, (dq_out, dk_out) = refs[:chunks], refs[chunks:-2], refs[-2:]
    total = parts[0][...]
    for ref in parts[1:]:
        total = total + ref[...].astype(F32)
    depth = dq_out.shape[2]
    for j in range(dq_out.shape[1]):
        dq_out[:, j, :] = total[:, j * depth : (j + 1) * depth]
    dk = dk_parts[0][...]
    for ref in dk_parts[1:]:
        dk = dk + ref[...].astype(F32)
    dk_out[...] = dk


def body(
    ctx,
    peers,
    query_heads,
    absorb_up,
    latent_keys,
    lse_heads,
    index_query,
    index_weight,
    index_keys,
    lse_index,
    query_pos,
    key_blocks,
):
    chunk, heads, width = query_heads.shape
    _, nope, latent = absorb_up.shape
    rope = width - nope
    keys = latent_keys.shape[0]
    index_heads, depth = index_query.shape[1:]
    count = chunk * ctx
    half = count // 2
    me = lax.axis_index("ctx")
    info = jnp.stack([key_blocks[0], lax.axis_index("head").astype(jnp.int32)])
    evens = list(range(2, ctx, 2))

    def gather(payload):
        side = jnp.concatenate([payload] + [send(payload, "ctx", ctx, k) for k in evens], axis=0)
        return side, send(side, "ctx", ctx, 1)

    index_a, index_b = gather(
        jnp.concatenate(
            [index_query.reshape(chunk, -1), jnp.pad(index_weight, ((0, 0), (0, LANES - index_heads)))],
            axis=1,
        )
    )
    side_a, side_b = gather(
        jnp.concatenate(
            [query_heads[:, :, :nope].reshape(chunk, -1), query_heads[:, :, nope:].reshape(chunk, -1)],
            axis=1,
        )
    )

    local = jnp.concatenate(
        [lse_heads * LOG2E, lse_index[:, None], query_pos.astype(F32)[:, None]], axis=1
    )
    local = in_local_order(local.reshape(ctx, chunk, -1), me).reshape(count, -1)
    group = min(8, heads)
    steps = heads // group
    lse_groups = jnp.swapaxes(local[:, :heads].reshape(count, steps, group), 0, 1)
    lse_column = local[:, heads : heads + 1]
    pos_column = local[:, heads + 1 : heads + 2].astype(jnp.int32)

    latent_t = jnp.pad(latent_keys, ((0, 0), (0, LANES - rope))).T
    index_t = index_keys.T

    iq_width = index_heads * depth
    iq_spec = pl.BlockSpec((half, iq_width), lambda *_: (0, 0))
    w_spec = pl.BlockSpec((half, LANES), lambda *_: (0, iq_width // LANES))
    part_rows = count // peers
    logit_slices = call(
        logit_kernel,
        [jax.ShapeDtypeStruct((part_rows, keys), F32)] * peers,
        grid=(1,),
        in_specs=[smem(), iq_spec, iq_spec, w_spec, w_spec, vmem()],
        out_specs=[vmem()] * peers,
        scratch_shapes=[pltpu.VMEM((index_heads * count, depth), BF16), pltpu.VMEM((count, keys), F32)],
    )(info, index_a, index_b, index_a, index_b, index_t)
    index_prob = call(
        index_prob_kernel,
        jax.ShapeDtypeStruct((part_rows, keys), BF16),
        in_specs=[smem()] + [vmem()] * (peers + 2),
        out_specs=vmem(),
    )(info, lse_column, pos_column, *swap_heads(logit_slices, peers))
    index_probs = swap_heads([index_prob] * peers, peers)

    rope_first = heads * nope // (group * rope)
    nope_spec = pl.BlockSpec((half, group * nope), lambda g: (0, g))
    rope_spec = pl.BlockSpec((half, group * rope), lambda g: (0, rope_first + g))
    slices = call(
        functools.partial(prob_kernel, width ** -0.5),
        [jax.ShapeDtypeStruct((part_rows, keys + count), BF16)] * peers,
        grid=(steps,),
        in_specs=[
            smem(),
            nope_spec,
            nope_spec,
            rope_spec,
            rope_spec,
            pl.BlockSpec((group, nope, latent), lambda g: (g, 0, 0)),
            vmem(),
            pl.BlockSpec((1, count, group), lambda g: (g, 0, 0)),
            vmem(),
        ],
        out_specs=[vmem()] * peers,
        scratch_shapes=[
            pltpu.VMEM((group * count, latent + LANES), BF16),
            pltpu.VMEM((count, keys), F32),
        ],
    )(info, side_a, side_b, side_a, side_b, absorb_up, latent_t, lse_groups, pos_column)

    merged, row_sum = call(
        merge_kernel,
        [jax.ShapeDtypeStruct((part_rows, keys), BF16), jax.ShapeDtypeStruct((8, count), F32)],
    )(*swap_heads(slices, peers))
    row_sum = call(
        functools.partial(add_swapped_kernel, chunk),
        jax.ShapeDtypeStruct((8, count), F32),
    )(row_sum, send(row_sum, "ctx", ctx, 1))
    totals = [row_sum] + [send(row_sum, "ctx", ctx, k) for k in evens]
    gathered = swap_heads([merged] * peers, peers)

    loss_scale = (keys * ctx) ** 0.5
    dk_slice = (keys // peers, depth)
    outs = call(
        functools.partial(grad_kernel, loss_scale, chunk, peers, evens),
        [
            jax.ShapeDtypeStruct((half, iq_width), F32),
            jax.ShapeDtypeStruct((half, iq_width), BF16),
            jax.ShapeDtypeStruct(dk_slice, F32),
        ]
        + [jax.ShapeDtypeStruct(dk_slice, BF16)] * (peers - 1),
        grid=(1,),
        in_specs=[smem()]
        + [vmem()] * (2 * peers + len(totals))
        + [iq_spec, iq_spec, w_spec, w_spec, vmem(), vmem()],
        out_specs=[vmem()] * (peers + 2),
        scratch_shapes=[
            pltpu.VMEM((index_heads * count, depth), BF16),
            pltpu.VMEM((count, keys), F32),
            pltpu.VMEM((keys, depth), F32),
        ],
    )(
        info,
        *gathered,
        *index_probs,
        *totals,
        index_a,
        index_b,
        index_a,
        index_b,
        index_keys,
        index_t,
    )
    keep, away, dk_own, *dk_away = outs
    other = send(away, "ctx", ctx, 1)
    dk_parts = swap_heads([dk_own] + dk_away, peers)
    own, *parts = call(
        fold_kernel,
        [jax.ShapeDtypeStruct((chunk, iq_width), F32)]
        + [jax.ShapeDtypeStruct((chunk, iq_width), BF16)] * len(evens),
    )(keep, other)
    dq_parts = [own] + [send(part, "ctx", ctx, k) for part, k in zip(parts, evens)]
    return tuple(
        call(
            functools.partial(final_kernel, len(dq_parts)),
            [
                jax.ShapeDtypeStruct((chunk, index_heads, depth), F32),
                jax.ShapeDtypeStruct(dk_slice, F32),
            ],
        )(*dq_parts, *dk_parts)
    )


def solution(mesh):
    placed = (
        P("ctx", "head", None),
        P("head", None, None),
        P("ctx", None),
        P(None, "head"),
        P("ctx", "head", None),
        P("ctx", "head"),
        P("ctx", None),
        P(),
        P(),
        P("ctx"),
    )
    return jax.shard_map(
        functools.partial(body, mesh.shape["ctx"], mesh.shape["head"]),
        mesh=mesh,
        in_specs=placed,
        out_specs=(P("ctx", "head", None), P(("ctx", "head"), None)),
        check_vma=False,
    )
```

```python
import functools
import math

import jax
import jax.numpy as jnp
from jax import lax
from jax.experimental import pallas as pl
from jax.experimental.pallas import tpu as pltpu
from jax.sharding import PartitionSpec as P

LOG2E = math.log2(math.e)
F32 = jnp.float32
BF16 = jnp.bfloat16
LANES = 128
VMEM_LIMIT = 48 * 1024 * 1024


def matmul(lhs, rhs):
    return jnp.dot(lhs, rhs, preferred_element_type=F32)


def send(array, axis, size, offset):
    return lax.ppermute(array, axis, [(i, i ^ offset) for i in range(size)])


def swap_heads(slices, peers):
    return [slices[0]] + [send(slices[k], "head", peers, k) for k in range(1, peers)]


def call(kernel, out_shape, **options):
    return pl.pallas_call(
        kernel,
        out_shape=out_shape,
        compiler_params=pltpu.CompilerParams(vmem_limit_bytes=VMEM_LIMIT),
        **options,
    )


def vmem():
    return pl.BlockSpec(memory_space=pltpu.VMEM)


def smem():
    return pl.BlockSpec(memory_space=pltpu.SMEM)


def flip(row, offset, chunk):
    width = row.shape[1]
    block = lax.broadcasted_iota(jnp.int32, row.shape, 1) // chunk
    bit = 0
    while offset >> bit:
        if (offset >> bit) & 1:
            stride = width // (2 * chunk) if bit == 0 else 1 << (bit - 1)
            ahead = pltpu.roll(row, width - stride * chunk, 1)
            back = pltpu.roll(row, stride * chunk, 1)
            row = jnp.where((block // stride) % 2 == 0, ahead, back)
        bit += 1
    return row


def in_local_order(blocks, me):
    ctx, tail = blocks.shape[0], blocks.shape[1:]
    stride = 1
    while stride < ctx:
        swapped = blocks.reshape((-1, 2, stride) + tail)[:, ::-1].reshape(blocks.shape)
        blocks = jnp.where((me // stride) % 2 == 1, swapped, blocks)
        stride *= 2
    return jnp.swapaxes(blocks.reshape((ctx // 2, 2) + tail), 0, 1).reshape(blocks.shape)


def logit_kernel(info, iq_a, iq_b, w_a, w_b, keys_t, *rest):
    outs, rows, acc = rest[:-2], rest[-2], rest[-1]
    count = acc.shape[0]
    depth = keys_t.shape[0]
    heads = iq_a.shape[1] // depth
    scale = depth ** -0.5
    weight = jnp.concatenate([w_a[...], w_b[...]], axis=0).astype(F32) * scale
    for j in range(heads):
        part = slice(j * depth, (j + 1) * depth)
        rows[j * count : (j + 1) * count, :] = jnp.concatenate([iq_a[:, part], iq_b[:, part]], axis=0)
    group = min(4, heads)
    for first in range(0, heads, group):
        score = matmul(rows[first * count : (first + group) * count, :], keys_t[...])
        total = None
        for i in range(group):
            j = first + i
            term = weight[:, j : j + 1] * jnp.maximum(score[i * count : (i + 1) * count], 0.0)
            total = term if total is None else total + term
        if first == 0:
            acc[...] = total
        else:
            acc[...] += total
    size = count // len(outs)
    for k, out in enumerate(outs):
        start = pl.multiple_of(jnp.bitwise_xor(info[1], k) * size, size)
        out[...] = acc[pl.ds(start, size), :]


def prob_kernel(scale, info, na, nb, ra, rb, up, keys_t, lse, pos, *rest):
    outs, lhs, acc = rest[:-2], rest[-2], rest[-1]
    step = pl.program_id(0)
    group, depth, latent = up.shape
    count, keys = acc.shape
    rope = ra.shape[1] // group
    for i in range(group):
        part = slice(i * depth, (i + 1) * depth)
        query = jnp.concatenate([na[:, part], nb[:, part]], axis=0)
        lhs[i * count : (i + 1) * count, :latent] = matmul(query, up[i]).astype(BF16)
        low = (i * rope // LANES) * LANES
        pair = jnp.concatenate([ra[:, low : low + LANES], rb[:, low : low + LANES]], axis=0)
        shift = i * rope - low
        if shift:
            pair = jnp.concatenate([pair[:, shift:], pair[:, :shift]], axis=1)
        lhs[i * count : (i + 1) * count, latent:] = pair

    score = matmul(lhs[...], keys_t[...])
    total = None
    for i in range(group):
        term = jnp.exp2(score[i * count : (i + 1) * count] * (scale * LOG2E) - lse[0, :, i : i + 1])
        total = term if total is None else total + term

    @pl.when(step == 0)
    def _():
        acc[...] = total

    @pl.when(step > 0)
    def _():
        acc[...] += total

    @pl.when(step == pl.num_programs(0) - 1)
    def _():
        key_pos = info[0] * keys + lax.broadcasted_iota(jnp.int32, (count, keys), 1)
        masked = jnp.where(key_pos <= pos[...], acc[...], 0.0)
        acc[...] = masked
        total = jnp.sum(masked, axis=1, keepdims=True)
        size = count // len(outs)
        row = jnp.transpose(jnp.broadcast_to(total, (count, count)))[:size]
        line = lax.broadcasted_iota(jnp.int32, row.shape, 0)
        high = row.astype(BF16).astype(F32)
        middle = (row - high).astype(BF16).astype(F32)
        low = row - high - middle
        packed = jnp.where(line == 0, high, jnp.where(line == 1, middle, jnp.where(line == 2, low, 0.0)))
        for k, out in enumerate(outs):
            start = pl.multiple_of(jnp.bitwise_xor(info[1], k) * size, size)
            out[:, :keys] = acc[pl.ds(start, size), :].astype(BF16)
            out[:, keys:] = packed.astype(BF16)


def add_swapped_kernel(chunk, mine, other, out):
    out[...] = mine[...] + flip(other[...], 1, chunk)


def merge_kernel(*refs):
    slices, out, row_sum = refs[:-2], refs[-2], refs[-1]
    keys = out.shape[1]
    total = None
    for ref in slices:
        part = ref[...].astype(F32)
        total = part if total is None else total + part
    out[...] = total[:, :keys].astype(BF16)
    row = jnp.sum(total[:, keys:], axis=0, keepdims=True)
    row_sum[...] = jnp.broadcast_to(row, row_sum.shape)


def index_prob_kernel(info, lse, pos, *refs):
    slices, out = refs[:-1], refs[-1]
    size, keys = out.shape
    total = slices[0][...]
    for ref in slices[1:]:
        total = total + ref[...]
    rows = pl.ds(pl.multiple_of(info[1] * size, size), size)
    key_pos = info[0] * keys + lax.broadcasted_iota(jnp.int32, (size, keys), 1)
    out[...] = jnp.where(key_pos <= pos[rows, :], jnp.exp(total - lse[rows, :]), 0.0).astype(BF16)


def grad_kernel(loss_scale, chunk, peers, offsets, info, *refs):
    slices, refs = refs[:peers], refs[peers:]
    index_slices, refs = refs[:peers], refs[peers:]
    totals, refs = refs[: len(offsets) + 1], refs[len(offsets) + 1 :]
    iq_a, iq_b, w_a, w_b, index_keys, keys_t, keep, away = refs[:8]
    dk_outs, (rows, prob, dk, dk_rows) = refs[8:-4], refs[-4:]
    count, keys = prob.shape
    depth = keys_t.shape[0]
    heads = iq_a.shape[1] // depth
    half = count // 2
    scale = depth ** -0.5
    size = count // peers
    row = totals[0][...]
    for offset, ref in zip(offsets, totals[1:]):
        row = row + flip(ref[...], offset, chunk)
    square = (count, count)
    diagonal = lax.broadcasted_iota(jnp.int32, square, 0) == lax.broadcasted_iota(jnp.int32, square, 1)
    row_total = jnp.sum(jnp.where(diagonal, jnp.broadcast_to(row[:1], square), 0.0), axis=1, keepdims=True)
    prob[...] = jnp.broadcast_to(row_total, (count, keys))
    for k in range(peers):
        part = pl.ds(pl.multiple_of(jnp.bitwise_xor(info[1], k) * size, size), size)
        target = slices[k][...].astype(F32) / prob[part, :]
        prob[part, :] = loss_scale * (index_slices[k][...].astype(F32) - target)

    weight = jnp.concatenate([w_a[...], w_b[...]], axis=0).astype(F32)
    for j in range(heads):
        part = slice(j * depth, (j + 1) * depth)
        rows[j * count : (j + 1) * count, :] = jnp.concatenate([iq_a[:, part], iq_b[:, part]], axis=0)
    group = min(4, heads)
    for first in range(0, heads, group):
        mine = rows[first * count : (first + group) * count, :]
        score = matmul(mine, keys_t[...])
        d_score = jnp.concatenate(
            [
                jnp.where(
                    score[i * count : (i + 1) * count] > 0.0,
                    weight[:, first + i : first + i + 1] * prob[...],
                    0.0,
                ).astype(BF16)
                for i in range(group)
            ],
            axis=0,
        )
        dq = matmul(d_score, index_keys[...]) * scale
        for i in range(group):
            part = slice((first + i) * depth, (first + i + 1) * depth)
            keep[:, part] = dq[i * count : i * count + half]
            away[:, part] = dq[i * count + half : (i + 1) * count].astype(BF16)
        term = lax.dot_general(mine, d_score, (((0,), (0,)), ((), ())), preferred_element_type=F32)
        if first == 0:
            dk[...] = term
        else:
            dk[...] += term
    dk_rows[...] = jnp.transpose(dk[...]) * scale
    size = keys // peers
    for k, out in enumerate(dk_outs):
        start = pl.multiple_of(jnp.bitwise_xor(info[1], k) * size, size)
        out[...] = dk_rows[pl.ds(start, size), :].astype(out.dtype)


def fold_kernel(keep, other, own, *outs):
    chunk = own.shape[0]
    total = keep[...] + other[...].astype(F32)
    own[...] = total[:chunk]
    for i, out in enumerate(outs):
        out[...] = total[(i + 1) * chunk : (i + 2) * chunk].astype(BF16)


def final_kernel(chunks, *refs):
    parts, dk_parts, (dq_out, dk_out) = refs[:chunks], refs[chunks:-2], refs[-2:]
    total = parts[0][...]
    for ref in parts[1:]:
        total = total + ref[...].astype(F32)
    depth = dq_out.shape[2]
    for j in range(dq_out.shape[1]):
        dq_out[:, j, :] = total[:, j * depth : (j + 1) * depth]
    dk = dk_parts[0][...]
    for ref in dk_parts[1:]:
        dk = dk + ref[...].astype(F32)
    dk_out[...] = dk


def body(
    ctx,
    peers,
    query_heads,
    absorb_up,
    latent_keys,
    lse_heads,
    index_query,
    index_weight,
    index_keys,
    lse_index,
    query_pos,
    key_blocks,
):
    chunk, heads, width = query_heads.shape
    _, nope, latent = absorb_up.shape
    rope = width - nope
    keys = latent_keys.shape[0]
    index_heads, depth = index_query.shape[1:]
    count = chunk * ctx
    half = count // 2
    me = lax.axis_index("ctx")
    info = jnp.stack([key_blocks[0], lax.axis_index("head").astype(jnp.int32)])
    evens = list(range(2, ctx, 2))

    def gather(payload):
        side = jnp.concatenate([payload] + [send(payload, "ctx", ctx, k) for k in evens], axis=0)
        return side, send(side, "ctx", ctx, 1)

    index_a, index_b = gather(
        jnp.concatenate(
            [index_query.reshape(chunk, -1), jnp.pad(index_weight, ((0, 0), (0, LANES - index_heads)))],
            axis=1,
        )
    )
    side_a, side_b = gather(
        jnp.concatenate(
            [query_heads[:, :, :nope].reshape(chunk, -1), query_heads[:, :, nope:].reshape(chunk, -1)],
            axis=1,
        )
    )

    local = jnp.concatenate(
        [lse_heads * LOG2E, lse_index[:, None], query_pos.astype(F32)[:, None]], axis=1
    )
    local = in_local_order(local.reshape(ctx, chunk, -1), me).reshape(count, -1)
    group = min(8, heads)
    steps = heads // group
    lse_groups = jnp.swapaxes(local[:, :heads].reshape(count, steps, group), 0, 1)
    lse_column = local[:, heads : heads + 1]
    pos_column = local[:, heads + 1 : heads + 2].astype(jnp.int32)

    latent_t = jnp.pad(latent_keys, ((0, 0), (0, LANES - rope))).T
    index_t = index_keys.T

    iq_width = index_heads * depth
    iq_spec = pl.BlockSpec((half, iq_width), lambda *_: (0, 0))
    w_spec = pl.BlockSpec((half, LANES), lambda *_: (0, iq_width // LANES))
    part_rows = count // peers
    logit_slices = call(
        logit_kernel,
        [jax.ShapeDtypeStruct((part_rows, keys), F32)] * peers,
        grid=(1,),
        in_specs=[smem(), iq_spec, iq_spec, w_spec, w_spec, vmem()],
        out_specs=[vmem()] * peers,
        scratch_shapes=[pltpu.VMEM((index_heads * count, depth), BF16), pltpu.VMEM((count, keys), F32)],
    )(info, index_a, index_b, index_a, index_b, index_t)
    index_prob = call(
        index_prob_kernel,
        jax.ShapeDtypeStruct((part_rows, keys), BF16),
        in_specs=[smem()] + [vmem()] * (peers + 2),
        out_specs=vmem(),
    )(info, lse_column, pos_column, *swap_heads(logit_slices, peers))
    index_probs = swap_heads([index_prob] * peers, peers)

    rope_first = heads * nope // (group * rope)
    nope_spec = pl.BlockSpec((half, group * nope), lambda g: (0, g))
    rope_spec = pl.BlockSpec((half, group * rope), lambda g: (0, rope_first + g))
    slices = call(
        functools.partial(prob_kernel, width ** -0.5),
        [jax.ShapeDtypeStruct((part_rows, keys + count), BF16)] * peers,
        grid=(steps,),
        in_specs=[
            smem(),
            nope_spec,
            nope_spec,
            rope_spec,
            rope_spec,
            pl.BlockSpec((group, nope, latent), lambda g: (g, 0, 0)),
            vmem(),
            pl.BlockSpec((1, count, group), lambda g: (g, 0, 0)),
            vmem(),
        ],
        out_specs=[vmem()] * peers,
        scratch_shapes=[
            pltpu.VMEM((group * count, latent + LANES), BF16),
            pltpu.VMEM((count, keys), F32),
        ],
    )(info, side_a, side_b, side_a, side_b, absorb_up, latent_t, lse_groups, pos_column)

    merged, row_sum = call(
        merge_kernel,
        [jax.ShapeDtypeStruct((part_rows, keys), BF16), jax.ShapeDtypeStruct((8, count), F32)],
    )(*swap_heads(slices, peers))
    row_sum = call(
        functools.partial(add_swapped_kernel, chunk),
        jax.ShapeDtypeStruct((8, count), F32),
    )(row_sum, send(row_sum, "ctx", ctx, 1))
    totals = [row_sum] + [send(row_sum, "ctx", ctx, k) for k in evens]
    gathered = swap_heads([merged] * peers, peers)

    loss_scale = (keys * ctx) ** 0.5
    dk_slice = (keys // peers, depth)
    outs = call(
        functools.partial(grad_kernel, loss_scale, chunk, peers, evens),
        [
            jax.ShapeDtypeStruct((half, iq_width), F32),
            jax.ShapeDtypeStruct((half, iq_width), BF16),
            jax.ShapeDtypeStruct(dk_slice, F32),
        ]
        + [jax.ShapeDtypeStruct(dk_slice, BF16)] * (peers - 1),
        grid=(1,),
        in_specs=[smem()]
        + [vmem()] * (2 * peers + len(totals))
        + [iq_spec, iq_spec, w_spec, w_spec, vmem(), vmem()],
        out_specs=[vmem()] * (peers + 2),
        scratch_shapes=[
            pltpu.VMEM((index_heads * count, depth), BF16),
            pltpu.VMEM((count, keys), F32),
            pltpu.VMEM((depth, keys), F32),
            pltpu.VMEM((keys, depth), F32),
        ],
    )(
        info,
        *gathered,
        *index_probs,
        *totals,
        index_a,
        index_b,
        index_a,
        index_b,
        index_keys,
        index_t,
    )
    keep, away, dk_own, *dk_away = outs
    other = send(away, "ctx", ctx, 1)
    dk_parts = swap_heads([dk_own] + dk_away, peers)
    own, *parts = call(
        fold_kernel,
        [jax.ShapeDtypeStruct((chunk, iq_width), F32)]
        + [jax.ShapeDtypeStruct((chunk, iq_width), BF16)] * len(evens),
    )(keep, other)
    dq_parts = [own] + [send(part, "ctx", ctx, k) for part, k in zip(parts, evens)]
    return tuple(
        call(
            functools.partial(final_kernel, len(dq_parts)),
            [
                jax.ShapeDtypeStruct((chunk, index_heads, depth), F32),
                jax.ShapeDtypeStruct(dk_slice, F32),
            ],
        )(*dq_parts, *dk_parts)
    )


def solution(mesh):
    placed = (
        P("ctx", "head", None),
        P("head", None, None),
        P("ctx", None),
        P(None, "head"),
        P("ctx", "head", None),
        P("ctx", "head"),
        P("ctx", None),
        P(),
        P(),
        P("ctx"),
    )
    return jax.shard_map(
        functools.partial(body, mesh.shape["ctx"], mesh.shape["head"]),
        mesh=mesh,
        in_specs=placed,
        out_specs=(P("ctx", "head", None), P(("ctx", "head"), None)),
        check_vma=False,
    )
```
